32 devices in a mesh: grp: 2 (over core), row: 4 (over y, x), col: 4 (over z).
Axes of the slice: x: 2, y: 2, z: 4, core: 2. Of those that a mesh axis runs over, the one named last changes fastest.
Arguments:
- velocity: bfloat16 [3, 64, 16, 512], P(None, None, ('row', 'col'), 'grp'), may hold values from -0.25 to 0.25
- density: float32 [64, 16, 2048], P(('row', 'col'), None, 'grp'), may hold values from -6 to 6
- live_planes: int32 [16], P(('row', 'col')), may hold values from 1 to 4, 32 in all
Outputs:
- density_next: float32 [64, 16, 2048], P(('row', 'col'), None, 'grp')
- buoyancy: float32 [64, 16, 512], P(None, ('row', 'col'), 'grp')
The draws below stay inside these ranges and needn't reach their ends.
Inputs may be any that keep to these rules, and one draw needn't show every extreme that they name: live_planes[s] counts the planes of slab s, from its first plane on, that are advanced; the counts sum to 32 and one of them equals 4.
All inputs are finite; a program needn't handle non-finite values. No bound on the sum of `live_planes` on one device may be relied on, other than what follows from the above.
Results may differ from the reference program's by a relative error of at most 0.0035.
Values may be sent and summed in bfloat16 or wider, within the bound.
No kernel may reach another device: no remote copies, remote signals or barrier semaphores. Data moves between devices by JAX's collectives and lax.ppermute only.
A program may use at most 128 MiB of HBM per device.

```python
import math
import jax
import jax.numpy as jnp
import numpy as np
from jax import lax

NC = 512
NF = 2048
PLANES = 4
SLABS = 16
NZ = 64
NY = 16


def block_levels(rng, shape, split, least, largest):
    def one(position, parts):
        draws = jax.random.uniform(jax.random.fold_in(jax.random.fold_in(rng, 6), position), (parts,), jnp.float32, least / len(split), largest / len(split))
        return jnp.repeat(jnp.exp(draws), shape[position] // parts).reshape((-1,) + (1,) * (len(shape) - position - 1))

    level = one(*split[0])
    for cut in split[1:]:
        level = level * one(*cut)
    return level


def split_up(count, total, most, lean):
    weights = [(1 << 20) // math.isqrt(rank ** lean) + 1 for rank in range(2, count + 1)]
    spare, given = total - most - (count - 1), [1] * (count - 1)
    while spare > 0:
        candidates = [i for i in range(count - 1) if given[i] < most]
        pool, remaining = sum([weights[i] for i in candidates]), spare
        for i in candidates:
            addition = min(most - given[i], max(1, remaining * weights[i] // pool), spare)
            given[i] = given[i] + addition
            spare = spare - addition
    return np.array([most] + given)


def uneven(rng, number_of, total, limit, lean):
    if number_of == 2:
        one = jax.random.randint(rng, (), max(1, total - limit), min(limit, total - 1) + 1)
        return jnp.stack([one, total - one])
    sizes = jnp.asarray(split_up(number_of, total, limit, lean), jnp.int32)
    pairs = (number_of - 1) // 2
    source_of, sink = sizes[1:1 + 2 * pairs:2], sizes[2:2 + 2 * pairs:2]
    room = jnp.minimum(source_of - 1, limit - sink)
    passed = jax.random.randint(jax.random.fold_in(rng, 1), (pairs,), 0, 1 << 20) % (room + 1)
    sizes = sizes.at[1:1 + 2 * pairs:2].set(source_of - passed).at[2:2 + 2 * pairs:2].set(sink + passed)
    return sizes[jax.random.permutation(jax.random.fold_in(rng, 2), number_of)]


def gaussian(key, extent, width, limit, pieces=(), kind=jnp.bfloat16):
    gain = block_levels(key, extent, pieces, -0.22, 0.18) if pieces else 1.0
    array = jax.random.normal(key, extent, jnp.float32) * width * gain
    return jnp.minimum(jnp.maximum(array, -limit), limit).astype(kind)


def setup_inputs(seed: int = 0) -> dict:
    splits = jax.random.split(jax.random.key(seed), 4)
    velocity = gaussian(splits[0], (3, NZ, NY, NC), NC ** -0.5, 0.25, ((2, 16), (3, 2)))
    density = gaussian(splits[1], (NZ, NY, NF), 1.0, 6.0, ((0, 16), (2, 2)), jnp.float32)
    live_planes = uneven(splits[2], SLABS, SLABS * PLANES // 2, PLANES, 2).astype(jnp.int32)
    return dict(velocity=velocity, density=density, live_planes=live_planes)


first_coef = (4.0 / 5.0, -1.0 / 5.0, 4.0 / 105.0, -1.0 / 280.0)
second_coef = (8.0 / 5.0, -1.0 / 5.0, 8.0 / 315.0, -1.0 / 560.0)
centre_coef = -205.0 / 72.0
kappa_value = 0.1
step_value = 0.2
strat_value = 1.0

def basis_rows(mode_count, fine_cells, first_cell, cell_count):
    index_k = jnp.arange(mode_count, dtype=jnp.int32)
    index_i = first_cell + jnp.arange(cell_count, dtype=jnp.int32)
    half_modes = mode_count // 2
    frequency = jnp.where(index_k < half_modes, index_k, index_k - half_modes + 1)
    phase = frequency[:, None] * index_i[None, :] % fine_cells
    angle = phase.astype(jnp.float32) * (2.0 * math.pi / fine_cells)
    table = jnp.where((index_k < half_modes)[:, None], jnp.cos(angle), jnp.sin(angle))
    return table.astype(jnp.bfloat16)

def tendency(field, along_x, along_z, fine_velocity):
    plane_count = field.shape[0]
    cell_count = field.shape[2]
    grad_x = jnp.zeros_like(field)
    grad_y = jnp.zeros_like(field)
    grad_z = jnp.zeros_like(field)
    laplace = 3.0 * centre_coef * field
    for reach in range(1, 5):
        ahead = along_x[:, :, 4 + reach:4 + reach + cell_count]
        behind = along_x[:, :, 4 - reach:4 - reach + cell_count]
        grad_x = grad_x + first_coef[reach - 1] * (ahead - behind)
        laplace = laplace + second_coef[reach - 1] * (ahead + behind)
        ahead = jnp.roll(field, -reach, axis=1)
        behind = jnp.roll(field, reach, axis=1)
        grad_y = grad_y + first_coef[reach - 1] * (ahead - behind)
        laplace = laplace + second_coef[reach - 1] * (ahead + behind)
        ahead = along_z[4 + reach:4 + reach + plane_count]
        behind = along_z[4 - reach:4 - reach + plane_count]
        grad_z = grad_z + first_coef[reach - 1] * (ahead - behind)
        laplace = laplace + second_coef[reach - 1] * (ahead + behind)
    vel_u = fine_velocity[0]
    vel_v = fine_velocity[1]
    vel_w = fine_velocity[2]
    advect = vel_u * grad_x + vel_v * grad_y + vel_w * grad_z
    return kappa_value * laplace - advect - strat_value * vel_w

def reference(velocity, density, live_planes):
    table = basis_rows(NC, NF, 0, NF)
    slab_ids = jnp.arange(SLABS, dtype=jnp.int32)

    def one_slab(slab):
        first_plane = slab * PLANES
        coarse = lax.dynamic_slice_in_dim(velocity, first_plane, PLANES, 1)
        fine_velocity = jnp.dot(coarse.reshape(-1, NC), table, preferred_element_type=jnp.float32)
        fine_velocity = fine_velocity.reshape(3, PLANES, NY, NF)
        plane_index = (first_plane - 4 + jnp.arange(PLANES + 8, dtype=jnp.int32)) % NZ
        along_z = jnp.take(density, plane_index, axis=0)
        field = along_z[4:4 + PLANES]
        along_x = jnp.concatenate([field[:, :, NF - 4:], field, field[:, :, :4]], axis=2)
        change = tendency(field, along_x, along_z, fine_velocity)
        active = (jnp.arange(PLANES, dtype=jnp.int32) < live_planes[slab])[:, None, None]
        advanced = jnp.where(active, field + step_value * change, field)
        coarse_density = advanced.astype(jnp.bfloat16)
        product = lax.dot_general(coarse_density.reshape(-1, NF), table, (((1,), (1,)), ((), ())), preferred_element_type=jnp.float32)
        lifted = -math.sqrt(2.0 / NF) * product.reshape(PLANES, NY, NC)
        return (advanced, lifted)
    advanced_all, lifted_all = lax.map(one_slab, slab_ids)
    return (advanced_all.reshape(NZ, NY, NF), lifted_all.reshape(NZ, NY, NC))
```

```python
import functools
import math

import jax
import jax.numpy as jnp
import numpy as np
from jax import lax
from jax.experimental import pallas as pl
from jax.experimental.pallas import tpu as pltpu
from jax.sharding import PartitionSpec as P

first_coef = (4.0 / 5.0, -1.0 / 5.0, 4.0 / 105.0, -1.0 / 280.0)
second_coef = (8.0 / 5.0, -1.0 / 5.0, 8.0 / 315.0, -1.0 / 560.0)
centre_coef = -205.0 / 72.0
kappa_value = 0.1
step_value = 0.2
strat_value = 1.0

LANES = 128
GROUP = 16
ALL = ("grp", "row", "col")


def half_table(mode_count, fine_cells):
    k = np.arange(mode_count)
    half = mode_count // 2
    frequency = np.where(k < half, k, k - half + 1)
    phase = frequency[:, None] * np.arange(fine_cells // 2)[None, :] % fine_cells
    angle = phase.astype(np.float32) * np.float32(2.0 * math.pi / fine_cells)
    table = np.where((k < half)[:, None], np.cos(angle), np.sin(angle)).astype(np.float32)
    order = k.reshape(2, half // LANES, LANES).transpose(1, 0, 2).reshape(-1)
    sign = np.where(frequency % 2 == 0, 1.0, -1.0)
    return table[order].astype(jnp.bfloat16), sign[order].astype(np.float32)[None, :]


def selector(out_axes, in_axes, sizes):
    count = math.prod(sizes[a] for a in in_axes)
    index = np.arange(count).reshape([sizes[a] for a in in_axes])
    source = index.transpose([in_axes.index(a) for a in out_axes]).reshape(-1)
    matrix = np.zeros((count, count), np.float32)
    matrix[np.arange(count), source] = 1.0
    return matrix.astype(jnp.bfloat16)


def exact(matrix, rows):
    return jnp.dot(matrix, rows, preferred_element_type=jnp.float32).astype(jnp.bfloat16)


def prepare_kernel(planes, vel_ref, dens_ref, mat_ref, send_ref, dens16_ref, edge_ref):
    comps, depth, modes = vel_ref.shape
    tiles = modes // LANES
    step = GROUP * planes
    chunk = comps * planes * tiles * GROUP
    for b in range(depth // step):
        parts = []
        for c in range(comps):
            rows = vel_ref[c, pl.ds(b * step, step), :]
            for h in range(tiles):
                parts.append(rows[:, h * LANES : (h + 1) * LANES])
        mixed = exact(mat_ref[...], jnp.concatenate(parts, axis=0))
        send_ref[0, pl.ds(b * chunk, chunk), :] = mixed
        send_ref[1, pl.ds(b * chunk, chunk), :] = mixed
    cells = dens_ref.shape[2]
    for p in range(planes):
        field = dens_ref[p]
        dens16_ref[p] = field.astype(jnp.bfloat16)
        lane = lax.broadcasted_iota(jnp.int32, (field.shape[0], LANES), 1)
        edge_ref[p] = jnp.where(lane < LANES // 2, field[:, :LANES], field[:, cells - LANES :])


def stencil_kernel(dens_ref, low_ref, high_ref, edge_ref, gx_ref, gy_ref, gz_ref, base_ref, zz_ref):
    planes, rows, cells = dens_ref.shape
    zz_ref[pl.ds(0, planes)] = low_ref[...].astype(jnp.float32)
    zz_ref[pl.ds(planes, planes)] = dens_ref[...]
    zz_ref[pl.ds(2 * planes, planes)] = high_ref[...].astype(jnp.float32)

    def one(p):
        field = dens_ref[p]
        wide = jnp.concatenate([field, edge_ref[p]], axis=1)
        span = wide.shape[1]
        grad_x = grad_y = grad_z = lap = None
        for reach in range(1, 5):
            ahead_x = pltpu.roll(wide, span - reach, 1)[:, :cells]
            behind_x = pltpu.roll(wide, reach, 1)[:, :cells]
            ahead_y = pltpu.roll(field, rows - reach, 0)
            behind_y = pltpu.roll(field, reach, 0)
            ahead_z = zz_ref[p + planes + reach]
            behind_z = zz_ref[p + planes - reach]
            a = step_value * first_coef[reach - 1]
            b = step_value * kappa_value * second_coef[reach - 1]
            total = (ahead_x + behind_x) + (ahead_y + behind_y) + (ahead_z + behind_z)
            if reach == 1:
                grad_x = a * (ahead_x - behind_x)
                grad_y = a * (ahead_y - behind_y)
                grad_z = a * (ahead_z - behind_z) + step_value * strat_value
                lap = (1.0 + step_value * kappa_value * 3.0 * centre_coef) * field + b * total
            else:
                grad_x = grad_x + a * (ahead_x - behind_x)
                grad_y = grad_y + a * (ahead_y - behind_y)
                grad_z = grad_z + a * (ahead_z - behind_z)
                lap = lap + b * total
        gx_ref[p] = grad_x
        gy_ref[p] = grad_y
        gz_ref[p] = grad_z
        base_ref[p] = lap

    loop_planes(planes, rows, one)


def loop_planes(planes, rows, body):
    if rows <= GROUP:
        for p in range(planes):
            body(p)
    else:
        lax.fori_loop(0, planes, lambda p, _: (body(p), 0)[1], 0)


def advance_kernel(
    scale, live_ref, side_ref, recv_ref, table_ref, sign_ref, in_mat_ref, out_mat_ref,
    dens_ref, gx_ref, gy_ref, gz_ref, base_ref, next_ref, send_ref, fine_ref,
):
    planes, rows, cells = dens_ref.shape
    modes = table_ref.shape[0]
    tiles = modes // (2 * LANES)
    comps = 3
    chunk = comps * planes * tiles * GROUP
    per_tile = chunk // tiles
    sign = jnp.where(side_ref[0] == 0, jnp.ones_like(sign_ref[...]), sign_ref[...])
    back = GROUP * planes * tiles
    for b in range(rows // GROUP):
        lanes = [recv_ref[g, pl.ds(b * chunk, chunk), :] for g in range(2)]
        mixed = jnp.dot(
            in_mat_ref[...], jnp.concatenate(lanes, axis=1), preferred_element_type=jnp.float32
        )
        coarse = jnp.concatenate(
            [mixed[h * per_tile : (h + 1) * per_tile] for h in range(tiles)], axis=1
        )
        coarse = (coarse * sign).astype(jnp.bfloat16)
        fine_ref[...] = jnp.dot(coarse, table_ref[...], preferred_element_type=jnp.float32)
        here = pl.ds(b * GROUP, GROUP)
        parts = []
        for p in range(planes):
            vel = [fine_ref[pl.ds((c * planes + p) * GROUP, GROUP), :] for c in range(comps)]
            moved = base_ref[p, here, :] - (
                vel[0] * gx_ref[p, here, :] + vel[1] * gy_ref[p, here, :] + vel[2] * gz_ref[p, here, :]
            )
            value = jnp.where(p < live_ref[0], moved, dens_ref[p, here, :])
            next_ref[p, here, :] = value
            parts.append(value.astype(jnp.bfloat16))
        lifted = lax.dot_general(
            jnp.concatenate(parts, axis=0), table_ref[...], (((1,), (1,)), ((), ())),
            preferred_element_type=jnp.float32,
        )
        lifted = (lifted * (sign * scale)).astype(jnp.bfloat16)
        stacked = jnp.concatenate(
            [lifted[:, h * 2 * LANES : (h + 1) * 2 * LANES] for h in range(tiles)], axis=0
        )
        ordered = exact(out_mat_ref[...], stacked)
        for g in range(2):
            send_ref[g, pl.ds(b * back, back), :] = ordered[:, g * LANES : (g + 1) * LANES]


def per_device(velocity, density, live_planes):
    comps, depth, _, modes = velocity.shape
    planes, rows, cells = density.shape
    slabs = depth // planes
    tiles = modes // LANES
    fine_cells = 2 * cells
    table, sign = half_table(2 * modes, fine_cells)
    sizes = dict(s=GROUP, c=comps, p=planes, h=tiles, y=GROUP)
    prep_mat = selector("shcp", "chsp", sizes)
    in_mat = selector("hcpy", "yhcp", sizes)
    out_mat = selector("yph", "hpy", sizes)
    chunk = comps * planes * tiles
    vmem = pl.BlockSpec(memory_space=pltpu.VMEM)
    smem = pl.BlockSpec(memory_space=pltpu.SMEM)
    params = pltpu.CompilerParams(vmem_limit_bytes=(24 if rows <= GROUP else 56) * 2**20)
    f32, b16 = jnp.float32, jnp.bfloat16

    send, dens16, edge = pl.pallas_call(
        functools.partial(prepare_kernel, planes),
        out_shape=(
            jax.ShapeDtypeStruct((2, slabs * chunk, LANES), b16),
            jax.ShapeDtypeStruct(density.shape, b16),
            jax.ShapeDtypeStruct((planes, rows, LANES), f32),
        ),
        in_specs=[vmem] * 3,
        out_specs=(vmem,) * 3,
        compiler_params=params,
        name="prepare",
    )(velocity.reshape(comps, depth, modes), density, prep_mat)

    count = slabs
    forward = [(i, (i + 1) % count) for i in range(count)]
    backward = [(target, source) for source, target in forward]
    other = lax.ppermute(edge, "grp", [(0, 1), (1, 0)])
    low = lax.ppermute(dens16, ("row", "col"), forward)
    high = lax.ppermute(dens16, ("row", "col"), backward)
    recv = lax.all_to_all(send.reshape(2 * slabs, chunk, LANES), ALL, 0, 0, tiled=True)
    recv = recv.reshape(2, slabs * chunk, LANES)

    field = jax.ShapeDtypeStruct(density.shape, f32)
    grads = pl.pallas_call(
        stencil_kernel,
        out_shape=(field,) * 4,
        in_specs=[vmem] * 4,
        out_specs=(vmem,) * 4,
        scratch_shapes=[pltpu.VMEM((3 * planes, rows, cells), f32)],
        compiler_params=params,
        cost_estimate=pl.CostEstimate(flops=60 * density.size, bytes_accessed=24 * density.size, transcendentals=0),
        name="stencil",
    )(density, low, high, other)

    side = lax.axis_index("grp").reshape(1)
    scale = -math.sqrt(2.0 / fine_cells)
    density_next, back = pl.pallas_call(
        functools.partial(advance_kernel, scale),
        out_shape=(field, jax.ShapeDtypeStruct((2, rows * planes * tiles, LANES), b16)),
        in_specs=[smem, smem] + [vmem] * 10,
        out_specs=(vmem,) * 2,
        scratch_shapes=[pltpu.VMEM((comps * planes * GROUP, cells), f32)],
        compiler_params=params,
        name="advance",
    )(live_planes, side, recv, table, sign, in_mat, out_mat, density, *grads)

    home = lax.all_to_all(back.reshape(2 * rows, planes * tiles, LANES), ALL, 0, 0, tiled=True)
    home = home.reshape(2, slabs * planes * tiles, LANES).astype(f32)
    buoyancy = (home[0] + home[1]).reshape(depth, 1, modes)
    return (density_next, buoyancy)


def solution(mesh):
    in_specs = (
        P(None, None, ("row", "col"), "grp"),
        P(("row", "col"), None, "grp"),
        P(("row", "col")),
    )
    out_specs = (P(("row", "col"), None, "grp"), P(None, ("row", "col"), "grp"))
    return jax.shard_map(
        per_device, mesh=mesh, in_specs=in_specs, out_specs=out_specs, check_vma=False
    )
```

```python
import functools
import math

import jax
import jax.numpy as jnp
import numpy as np
from jax import lax
from jax.experimental import pallas as pl
from jax.experimental.pallas import tpu as pltpu
from jax.sharding import PartitionSpec as P

first_coef = (4.0 / 5.0, -1.0 / 5.0, 4.0 / 105.0, -1.0 / 280.0)
second_coef = (8.0 / 5.0, -1.0 / 5.0, 8.0 / 315.0, -1.0 / 560.0)
centre_coef = -205.0 / 72.0
kappa_value = 0.1
step_value = 0.2
strat_value = 1.0

LANES = 128
GROUP = 16
ALL = ("grp", "row", "col")
STENCIL_FLOPS = 2 * 10**10


def half_tables(mode_count, fine_cells):
    k = np.arange(mode_count)
    half = mode_count // 2
    frequency = np.where(k < half, k, k - half + 1)
    phase = frequency[:, None] * np.arange(fine_cells)[None, :] % fine_cells
    angle = phase.astype(np.float32) * np.float32(2.0 * math.pi / fine_cells)
    table = np.where((k < half)[:, None], np.cos(angle), np.sin(angle)).astype(np.float32)
    order = k.reshape(2, half // LANES, LANES).transpose(1, 0, 2).reshape(-1)
    table = table[order].reshape(mode_count, 2, fine_cells // 2).transpose(1, 0, 2)
    return np.ascontiguousarray(table).astype(jnp.bfloat16)


def selector(out_axes, in_axes, sizes):
    count = math.prod(sizes[a] for a in in_axes)
    index = np.arange(count).reshape([sizes[a] for a in in_axes])
    source = index.transpose([in_axes.index(a) for a in out_axes]).reshape(-1)
    matrix = np.zeros((count, count), np.float32)
    matrix[np.arange(count), source] = 1.0
    return matrix.astype(jnp.bfloat16)


def exact(matrix, rows):
    return jnp.dot(matrix, rows, preferred_element_type=jnp.float32).astype(jnp.bfloat16)


def prepare_kernel(
    planes, vel_hbm, dens_hbm, mat_hbm, send_ref, dens16_ref, edge_ref,
    vel_ref, dens_ref, mat_ref, sems,
):
    copies = [
        pltpu.make_async_copy(source, target, sems.at[i])
        for i, (source, target) in enumerate(
            [(dens_hbm, dens_ref), (vel_hbm, vel_ref), (mat_hbm, mat_ref)]
        )
    ]
    for copy in copies:
        copy.start()
    comps, depth, modes = vel_ref.shape
    tiles = modes // LANES
    step = GROUP * planes
    chunk = comps * planes * tiles * GROUP
    cells = dens_ref.shape[2]
    copies[0].wait()
    for p in range(planes):
        field = dens_ref[p]
        dens16_ref[p] = field.astype(jnp.bfloat16)
        lane = lax.broadcasted_iota(jnp.int32, (field.shape[0], LANES), 1)
        edge_ref[p] = jnp.where(lane < LANES // 2, field[:, :LANES], field[:, cells - LANES :])
    copies[1].wait()
    copies[2].wait()
    for b in range(depth // step):
        parts = []
        for c in range(comps):
            rows = vel_ref[c, pl.ds(b * step, step), :]
            for h in range(tiles):
                parts.append(rows[:, h * LANES : (h + 1) * LANES])
        mixed = exact(mat_ref[...], jnp.concatenate(parts, axis=0))
        send_ref[0, pl.ds(b * chunk, chunk), :] = mixed
        send_ref[1, pl.ds(b * chunk, chunk), :] = mixed


def stencil_kernel(
    side_ref, dens_hbm, low_ref, high_ref, edge_ref, table_hbm, in_hbm, out_hbm,
    gx_ref, gy_ref, gz_ref, base_ref, field_ref, table_ref, in_ref, out_ref, zz_ref, sems,
):
    planes, rows, cells = dens_hbm.shape
    copies = [
        pltpu.make_async_copy(source, target, sems.at[i])
        for i, (source, target) in enumerate(
            [
                (dens_hbm, field_ref), (table_hbm.at[side_ref[0]], table_ref),
                (in_hbm, in_ref), (out_hbm, out_ref),
            ]
        )
    ]
    for copy in copies:
        copy.start()
    zz_ref[pl.ds(0, planes)] = low_ref[...].astype(jnp.float32)
    zz_ref[pl.ds(2 * planes, planes)] = high_ref[...].astype(jnp.float32)
    copies[0].wait()
    zz_ref[pl.ds(planes, planes)] = field_ref[...]

    def one(p):
        field = field_ref[p]
        wide = jnp.concatenate([field, edge_ref[p]], axis=1)
        span = wide.shape[1]
        grad_x = grad_y = grad_z = lap = None
        for reach in range(1, 5):
            ahead_x = pltpu.roll(wide, span - reach, 1)[:, :cells]
            behind_x = pltpu.roll(wide, reach, 1)[:, :cells]
            ahead_y = pltpu.roll(field, rows - reach, 0)
            behind_y = pltpu.roll(field, reach, 0)
            ahead_z = zz_ref[p + planes + reach]
            behind_z = zz_ref[p + planes - reach]
            a = step_value * first_coef[reach - 1]
            b = step_value * kappa_value * second_coef[reach - 1]
            total = (ahead_x + behind_x) + (ahead_y + behind_y) + (ahead_z + behind_z)
            if reach == 1:
                grad_x = a * (ahead_x - behind_x)
                grad_y = a * (ahead_y - behind_y)
                grad_z = a * (ahead_z - behind_z) + step_value * strat_value
                lap = (1.0 + step_value * kappa_value * 3.0 * centre_coef) * field + b * total
            else:
                grad_x = grad_x + a * (ahead_x - behind_x)
                grad_y = grad_y + a * (ahead_y - behind_y)
                grad_z = grad_z + a * (ahead_z - behind_z)
                lap = lap + b * total
        gx_ref[p] = grad_x
        gy_ref[p] = grad_y
        gz_ref[p] = grad_z
        base_ref[p] = lap

    loop_planes(planes, rows, one)
    for copy in copies[1:]:
        copy.wait()


def loop_planes(planes, rows, body):
    if rows <= GROUP:
        for p in range(planes):
            body(p)
    else:
        lax.fori_loop(0, planes, lambda p, _: (body(p), 0)[1], 0)


def advance_kernel(
    scale, live_ref, recv_ref, table_ref, in_mat_ref, out_mat_ref,
    dens_ref, gx_ref, gy_ref, gz_ref, base_ref, next_hbm, send_ref, fine_ref, next_ref, sems,
):
    planes, rows, cells = dens_ref.shape
    modes = table_ref.shape[0]
    tiles = modes // (2 * LANES)
    comps = 3
    chunk = comps * planes * tiles * GROUP
    per_tile = chunk // tiles
    back = GROUP * planes * tiles
    groups = rows // GROUP
    copies = [
        pltpu.make_async_copy(next_ref.at[p], next_hbm.at[p], sems.at[p]) for p in range(planes)
    ]
    for b in range(groups):
        lanes = [recv_ref[g, pl.ds(b * chunk, chunk), :] for g in range(2)]
        mixed = exact(in_mat_ref[...], jnp.concatenate(lanes, axis=1))
        coarse = jnp.concatenate(
            [mixed[h * per_tile : (h + 1) * per_tile] for h in range(tiles)], axis=1
        )
        fine_ref[...] = jnp.dot(coarse, table_ref[...], preferred_element_type=jnp.float32)
        here = pl.ds(b * GROUP, GROUP)
        parts = []
        for p in range(planes):
            vel = [fine_ref[pl.ds((c * planes + p) * GROUP, GROUP), :] for c in range(comps)]
            moved = base_ref[p, here, :] - (
                vel[0] * gx_ref[p, here, :] + vel[1] * gy_ref[p, here, :] + vel[2] * gz_ref[p, here, :]
            )
            value = jnp.where(p < live_ref[0], moved, dens_ref[p, here, :])
            next_ref[p, here, :] = value
            if b == groups - 1:
                copies[p].start()
            parts.append(value.astype(jnp.bfloat16))
        lifted = lax.dot_general(
            jnp.concatenate(parts, axis=0), table_ref[...], (((1,), (1,)), ((), ())),
            preferred_element_type=jnp.float32,
        )
        lifted = (lifted * scale).astype(jnp.bfloat16)
        stacked = jnp.concatenate(
            [lifted[:, h * 2 * LANES : (h + 1) * 2 * LANES] for h in range(tiles)], axis=0
        )
        ordered = exact(out_mat_ref[...], stacked)
        for g in range(2):
            send_ref[g, pl.ds(b * back, back), :] = ordered[:, g * LANES : (g + 1) * LANES]
    for copy in copies:
        copy.wait()


def per_device(velocity, density, live_planes):
    comps, depth, _, modes = velocity.shape
    planes, rows, cells = density.shape
    slabs = depth // planes
    tiles = modes // LANES
    fine_cells = 2 * cells
    tables = half_tables(2 * modes, fine_cells)
    sizes = dict(s=GROUP, c=comps, p=planes, h=tiles, y=GROUP)
    prep_mat = selector("shcp", "chsp", sizes)
    in_mat = selector("hcpy", "yhcp", sizes)
    out_mat = selector("yph", "hpy", sizes)
    chunk = comps * planes * tiles
    vmem = pl.BlockSpec(memory_space=pltpu.VMEM)
    smem = pl.BlockSpec(memory_space=pltpu.SMEM)
    hbm = pl.BlockSpec(memory_space=pltpu.HBM)
    params = pltpu.CompilerParams(vmem_limit_bytes=(24 if rows <= GROUP else 56) * 2**20)
    f32, b16 = jnp.float32, jnp.bfloat16

    send, dens16, edge = pl.pallas_call(
        functools.partial(prepare_kernel, planes),
        out_shape=(
            jax.ShapeDtypeStruct((2, slabs * chunk, LANES), b16),
            jax.ShapeDtypeStruct(density.shape, b16),
            jax.ShapeDtypeStruct((planes, rows, LANES), f32),
        ),
        in_specs=[hbm] * 3,
        out_specs=(vmem,) * 3,
        scratch_shapes=[
            pltpu.VMEM((comps, depth, modes), b16),
            pltpu.VMEM(density.shape, f32),
            pltpu.VMEM(prep_mat.shape, b16),
            pltpu.SemaphoreType.DMA((3,)),
        ],
        compiler_params=params,
        name="prepare",
    )(velocity.reshape(comps, depth, modes), density, prep_mat)

    count = slabs
    forward = [(i, (i + 1) % count) for i in range(count)]
    backward = [(target, source) for source, target in forward]
    other = lax.ppermute(edge, "grp", [(0, 1), (1, 0)])
    low = lax.ppermute(dens16, ("row", "col"), forward)
    high = lax.ppermute(dens16, ("row", "col"), backward)
    recv = lax.all_to_all(send.reshape(2 * slabs, chunk, LANES), ALL, 0, 0, tiled=True)
    recv = recv.reshape(2, slabs * chunk, LANES)

    side = lax.axis_index("grp").reshape(1)
    field = jax.ShapeDtypeStruct(density.shape, f32)
    *grads, table, in_mat, out_mat = pl.pallas_call(
        stencil_kernel,
        out_shape=(field,) * 5 + tuple(
            jax.ShapeDtypeStruct(m.shape, b16) for m in (tables[0], in_mat, out_mat)
        ),
        in_specs=[smem, hbm, vmem, vmem, vmem, hbm, hbm, hbm],
        out_specs=(vmem,) * 8,
        scratch_shapes=[
            pltpu.VMEM((3 * planes, rows, cells), f32), pltpu.SemaphoreType.DMA((4,))
        ],
        compiler_params=params,
        cost_estimate=pl.CostEstimate(flops=STENCIL_FLOPS, bytes_accessed=24 * density.size, transcendentals=0),
        name="stencil",
    )(side, density, low, high, other, tables, in_mat, out_mat)
    gx, gy, gz, base, dens = grads

    scale = -math.sqrt(2.0 / fine_cells)
    density_next, back = pl.pallas_call(
        functools.partial(advance_kernel, scale),
        out_shape=(field, jax.ShapeDtypeStruct((2, rows * planes * tiles, LANES), b16)),
        in_specs=[smem] + [vmem] * 9,
        out_specs=(hbm, vmem),
        scratch_shapes=[
            pltpu.VMEM((comps * planes * GROUP, cells), f32),
            pltpu.VMEM(density.shape, f32),
            pltpu.SemaphoreType.DMA((planes,)),
        ],
        compiler_params=params,
        name="advance",
    )(live_planes, recv, table, in_mat, out_mat, dens, gx, gy, gz, base)

    home = lax.all_to_all(back.reshape(2 * rows, planes * tiles, LANES), ALL, 0, 0, tiled=True)
    home = home.reshape(2, slabs * planes * tiles, LANES).astype(f32)
    buoyancy = (home[0] + home[1]).reshape(depth, 1, modes)
    return (density_next, buoyancy)


def solution(mesh):
    in_specs = (
        P(None, None, ("row", "col"), "grp"),
        P(("row", "col"), None, "grp"),
        P(("row", "col")),
    )
    out_specs = (P(("row", "col"), None, "grp"), P(None, ("row", "col"), "grp"))
    return jax.shard_map(
        per_device, mesh=mesh, in_specs=in_specs, out_specs=out_specs, check_vma=False
    )
```

```python
import functools
import math

import jax
import jax.numpy as jnp
import numpy as np
from jax import lax
from jax.experimental import pallas as pl
from jax.experimental.pallas import tpu as pltpu
from jax.sharding import PartitionSpec as P

first_coef = (4.0 / 5.0, -1.0 / 5.0, 4.0 / 105.0, -1.0 / 280.0)
second_coef = (8.0 / 5.0, -1.0 / 5.0, 8.0 / 315.0, -1.0 / 560.0)
centre_coef = -205.0 / 72.0
kappa_value = 0.1
step_value = 0.2
strat_value = 1.0

LANES = 128
GROUP = 16
ALL = ("grp", "row", "col")
STENCIL_FLOPS = 2 * 10**10


def half_tables(mode_count, fine_cells):
    k = np.arange(mode_count)
    half = mode_count // 2
    frequency = np.where(k < half, k, k - half + 1)
    phase = frequency[:, None] * np.arange(fine_cells)[None, :] % fine_cells
    angle = phase.astype(np.float32) * np.float32(2.0 * math.pi / fine_cells)
    table = np.where((k < half)[:, None], np.cos(angle), np.sin(angle)).astype(np.float32)
    order = k.reshape(2, half // LANES, LANES).transpose(1, 0, 2).reshape(-1)
    table = table[order].reshape(mode_count, 2, fine_cells // 2).transpose(1, 0, 2)
    return np.ascontiguousarray(table).astype(jnp.bfloat16)


def selector(out_axes, in_axes, sizes):
    count = math.prod(sizes[a] for a in in_axes)
    index = np.arange(count).reshape([sizes[a] for a in in_axes])
    source = index.transpose([in_axes.index(a) for a in out_axes]).reshape(-1)
    matrix = np.zeros((count, count), np.float32)
    matrix[np.arange(count), source] = 1.0
    return matrix.astype(jnp.bfloat16)


def exact(matrix, rows):
    return jnp.dot(matrix, rows, preferred_element_type=jnp.float32).astype(jnp.bfloat16)


def keep(array):
    return pltpu.with_memory_space_constraint(array, pltpu.HBM)


def prepare_kernel(
    planes, vel_hbm, dens_hbm, mat_hbm, send_ref, dens16_ref, edge_ref,
    vel_ref, dens_ref, mat_ref, sems,
):
    copies = [
        pltpu.make_async_copy(source, target, sems.at[i])
        for i, (source, target) in enumerate(
            [(dens_hbm, dens_ref), (vel_hbm, vel_ref), (mat_hbm, mat_ref)]
        )
    ]
    for copy in copies:
        copy.start()
    comps, depth, modes = vel_ref.shape
    tiles = modes // LANES
    step = GROUP * planes
    chunk = comps * planes * tiles * GROUP
    cells = dens_ref.shape[2]
    copies[0].wait()
    for p in range(planes):
        field = dens_ref[p]
        dens16_ref[p] = field.astype(jnp.bfloat16)
        lane = lax.broadcasted_iota(jnp.int32, (field.shape[0], LANES), 1)
        edge_ref[p] = jnp.where(lane < LANES // 2, field[:, :LANES], field[:, cells - LANES :])
    copies[1].wait()
    copies[2].wait()
    for b in range(depth // step):
        parts = []
        for c in range(comps):
            rows = vel_ref[c, pl.ds(b * step, step), :]
            for h in range(tiles):
                parts.append(rows[:, h * LANES : (h + 1) * LANES])
        mixed = exact(mat_ref[...], jnp.concatenate(parts, axis=0))
        send_ref[0, pl.ds(b * chunk, chunk), :] = mixed
        send_ref[1, pl.ds(b * chunk, chunk), :] = mixed


def stencil_kernel(
    dens_hbm, near_ref, far_ref, edge_ref, table_hbm, in_hbm, out_hbm,
    gx_ref, gy_ref, gz_ref, base_ref, field_ref, table_ref, in_ref, out_ref, zz_ref, sems,
):
    planes, rows, cells = dens_hbm.shape
    copies = [
        pltpu.make_async_copy(source, target, sems.at[i])
        for i, (source, target) in enumerate(
            [
                (dens_hbm, field_ref), (table_hbm.at[lax.axis_index("grp")], table_ref),
                (in_hbm, in_ref), (out_hbm, out_ref),
            ]
        )
    ]
    for copy in copies:
        copy.start()
    odd = lax.axis_index(("row", "col")) % 2
    zz_ref[pl.ds(2 * planes * (1 - odd), planes)] = near_ref[...].astype(jnp.float32)
    zz_ref[pl.ds(2 * planes * odd, planes)] = far_ref[...].astype(jnp.float32)
    copies[0].wait()
    zz_ref[pl.ds(planes, planes)] = field_ref[...]

    def one(p):
        field = field_ref[p]
        wide = jnp.concatenate([field, edge_ref[p]], axis=1)
        span = wide.shape[1]
        grad_x = grad_y = grad_z = lap = None
        for reach in range(1, 5):
            ahead_x = pltpu.roll(wide, span - reach, 1)[:, :cells]
            behind_x = pltpu.roll(wide, reach, 1)[:, :cells]
            ahead_y = pltpu.roll(field, rows - reach, 0)
            behind_y = pltpu.roll(field, reach, 0)
            ahead_z = zz_ref[p + planes + reach]
            behind_z = zz_ref[p + planes - reach]
            a = step_value * first_coef[reach - 1]
            b = step_value * kappa_value * second_coef[reach - 1]
            total = (ahead_x + behind_x) + (ahead_y + behind_y) + (ahead_z + behind_z)
            if reach == 1:
                grad_x = a * (ahead_x - behind_x)
                grad_y = a * (ahead_y - behind_y)
                grad_z = a * (ahead_z - behind_z) + step_value * strat_value
                lap = (1.0 + step_value * kappa_value * 3.0 * centre_coef) * field + b * total
            else:
                grad_x = grad_x + a * (ahead_x - behind_x)
                grad_y = grad_y + a * (ahead_y - behind_y)
                grad_z = grad_z + a * (ahead_z - behind_z)
                lap = lap + b * total
        gx_ref[p] = grad_x
        gy_ref[p] = grad_y
        gz_ref[p] = grad_z
        base_ref[p] = lap

    loop_planes(planes, rows, one)
    for copy in copies[1:]:
        copy.wait()


def loop_planes(planes, rows, body):
    if rows <= GROUP:
        for p in range(planes):
            body(p)
    else:
        lax.fori_loop(0, planes, lambda p, _: (body(p), 0)[1], 0)


def advance_kernel(
    scale, live_ref, recv_ref, table_ref, in_mat_ref, out_mat_ref,
    dens_ref, gx_ref, gy_ref, gz_ref, base_ref, next_hbm, send_ref, fine_ref, next_ref, sems,
):
    planes, rows, cells = dens_ref.shape
    modes = table_ref.shape[0]
    tiles = modes // (2 * LANES)
    comps = 3
    chunk = comps * planes * tiles * GROUP
    per_tile = chunk // tiles
    back = GROUP * planes * tiles
    groups = rows // GROUP
    copies = [
        pltpu.make_async_copy(next_ref.at[p], next_hbm.at[p], sems.at[p]) for p in range(planes)
    ]
    for b in range(groups):
        lanes = [recv_ref[g, pl.ds(b * chunk, chunk), :] for g in range(2)]
        mixed = exact(in_mat_ref[...], jnp.concatenate(lanes, axis=1))
        coarse = jnp.concatenate(
            [mixed[h * per_tile : (h + 1) * per_tile] for h in range(tiles)], axis=1
        )
        fine_ref[...] = jnp.dot(coarse, table_ref[...], preferred_element_type=jnp.float32)
        here = pl.ds(b * GROUP, GROUP)
        parts = []
        for p in range(planes):
            vel = [fine_ref[pl.ds((c * planes + p) * GROUP, GROUP), :] for c in range(comps)]
            moved = base_ref[p, here, :] - (
                vel[0] * gx_ref[p, here, :] + vel[1] * gy_ref[p, here, :] + vel[2] * gz_ref[p, here, :]
            )
            value = jnp.where(p < live_ref[0], moved, dens_ref[p, here, :])
            next_ref[p, here, :] = value
            if b == groups - 1:
                copies[p].start()
            parts.append(value.astype(jnp.bfloat16))
        lifted = lax.dot_general(
            jnp.concatenate(parts, axis=0), table_ref[...], (((1,), (1,)), ((), ())),
            preferred_element_type=jnp.float32,
        )
        lifted = (lifted * scale).astype(jnp.bfloat16)
        stacked = jnp.concatenate(
            [lifted[:, h * 2 * LANES : (h + 1) * 2 * LANES] for h in range(tiles)], axis=0
        )
        ordered = exact(out_mat_ref[...], stacked)
        for g in range(2):
            send_ref[g, pl.ds(b * back, back), :] = ordered[:, g * LANES : (g + 1) * LANES]
    for copy in copies:
        copy.wait()


def per_device(velocity, density, live_planes):
    comps, depth, _, modes = velocity.shape
    planes, rows, cells = density.shape
    slabs = depth // planes
    tiles = modes // LANES
    fine_cells = 2 * cells
    tables = half_tables(2 * modes, fine_cells)
    sizes = dict(s=GROUP, c=comps, p=planes, h=tiles, y=GROUP)
    prep_mat = selector("shcp", "chsp", sizes)
    in_mat = selector("hcpy", "yhcp", sizes)
    out_mat = selector("yph", "hpy", sizes)
    chunk = comps * planes * tiles
    vmem = pl.BlockSpec(memory_space=pltpu.VMEM)
    smem = pl.BlockSpec(memory_space=pltpu.SMEM)
    hbm = pl.BlockSpec(memory_space=pltpu.HBM)
    params = pltpu.CompilerParams(vmem_limit_bytes=(24 if rows <= GROUP else 56) * 2**20)
    f32, b16 = jnp.float32, jnp.bfloat16

    send, dens16, edge = pl.pallas_call(
        functools.partial(prepare_kernel, planes),
        out_shape=(
            jax.ShapeDtypeStruct((2, slabs * chunk, LANES), b16),
            jax.ShapeDtypeStruct(density.shape, b16),
            jax.ShapeDtypeStruct((planes, rows, LANES), f32),
        ),
        in_specs=[hbm] * 3,
        out_specs=(vmem,) * 3,
        scratch_shapes=[
            pltpu.VMEM((comps, depth, modes), b16),
            pltpu.VMEM(density.shape, f32),
            pltpu.VMEM(prep_mat.shape, b16),
            pltpu.SemaphoreType.DMA((3,)),
        ],
        compiler_params=params,
        name="prepare",
    )(keep(velocity.reshape(comps, depth, modes)), keep(density), keep(prep_mat))

    count = slabs
    even_first = [(i, i ^ 1) for i in range(count)]
    odd_first = [((i + 1) % count, ((i ^ 1) + 1) % count) for i in range(count)]
    far = lax.ppermute(dens16, ("row", "col"), odd_first)
    near = lax.ppermute(dens16, ("row", "col"), even_first)
    other = lax.ppermute(edge, "grp", [(0, 1), (1, 0)])
    recv = lax.all_to_all(send.reshape(2 * slabs, chunk, LANES), ALL, 0, 0, tiled=True)
    recv = recv.reshape(2, slabs * chunk, LANES)

    field = jax.ShapeDtypeStruct(density.shape, f32)
    *grads, table, in_mat, out_mat = pl.pallas_call(
        stencil_kernel,
        out_shape=(field,) * 5 + tuple(
            jax.ShapeDtypeStruct(m.shape, b16) for m in (tables[0], in_mat, out_mat)
        ),
        in_specs=[hbm, vmem, vmem, vmem, hbm, hbm, hbm],
        out_specs=(vmem,) * 8,
        scratch_shapes=[
            pltpu.VMEM((3 * planes, rows, cells), f32), pltpu.SemaphoreType.DMA((4,))
        ],
        compiler_params=params,
        cost_estimate=pl.CostEstimate(flops=STENCIL_FLOPS, bytes_accessed=24 * density.size, transcendentals=0),
        name="stencil",
    )(keep(density), near, far, other, keep(tables), keep(in_mat), keep(out_mat))
    gx, gy, gz, base, dens = grads

    scale = -math.sqrt(2.0 / fine_cells)
    density_next, back = pl.pallas_call(
        functools.partial(advance_kernel, scale),
        out_shape=(field, jax.ShapeDtypeStruct((2, rows * planes * tiles, LANES), b16)),
        in_specs=[smem] + [vmem] * 9,
        out_specs=(hbm, vmem),
        scratch_shapes=[
            pltpu.VMEM((comps * planes * GROUP, cells), f32),
            pltpu.VMEM(density.shape, f32),
            pltpu.SemaphoreType.DMA((planes,)),
        ],
        compiler_params=params,
        name="advance",
    )(live_planes, recv, table, in_mat, out_mat, dens, gx, gy, gz, base)

    home = lax.all_to_all(back.reshape(2 * rows, planes * tiles, LANES), ALL, 0, 0, tiled=True)
    home = home.reshape(2, slabs * planes * tiles, LANES).astype(f32)
    buoyancy = (home[0] + home[1]).reshape(depth, 1, modes)
    return (density_next, buoyancy)


def solution(mesh):
    in_specs = (
        P(None, None, ("row", "col"), "grp"),
        P(("row", "col"), None, "grp"),
        P(("row", "col")),
    )
    out_specs = (P(("row", "col"), None, "grp"), P(None, ("row", "col"), "grp"))
    return jax.shard_map(
        per_device, mesh=mesh, in_specs=in_specs, out_specs=out_specs, check_vma=False
    )
```

```python
import functools
import math

import jax
import jax.numpy as jnp
import numpy as np
from jax import lax
from jax.experimental import pallas as pl
from jax.experimental.pallas import tpu as pltpu
from jax.sharding import PartitionSpec as P

first_coef = (4.0 / 5.0, -1.0 / 5.0, 4.0 / 105.0, -1.0 / 280.0)
second_coef = (8.0 / 5.0, -1.0 / 5.0, 8.0 / 315.0, -1.0 / 560.0)
centre_coef = -205.0 / 72.0
kappa_value = 0.1
step_value = 0.2
strat_value = 1.0

LANES = 128
GROUP = 16


def half_tables(mode_count, fine_cells):
    k = np.arange(mode_count)
    half = mode_count // 2
    frequency = np.where(k < half, k, k - half + 1)
    phase = frequency[:, None] * np.arange(fine_cells)[None, :] % fine_cells
    angle = phase.astype(np.float32) * np.float32(2.0 * math.pi / fine_cells)
    table = np.where((k < half)[:, None], np.cos(angle), np.sin(angle)).astype(np.float32)
    order = k.reshape(2, half // LANES, LANES).transpose(1, 0, 2).reshape(-1)
    table = table[order].reshape(mode_count, 2, fine_cells // 2).transpose(1, 0, 2)
    sign = np.where(frequency[order] % 2 == 0, 1.0, -1.0).astype(np.float32)
    return np.ascontiguousarray(table).astype(jnp.bfloat16), np.tile(sign, (8, 1))


def selector(out_axes, in_axes, sizes):
    count = math.prod(sizes[a] for a in in_axes)
    index = np.arange(count).reshape([sizes[a] for a in in_axes])
    source = index.transpose([in_axes.index(a) for a in out_axes]).reshape(-1)
    matrix = np.zeros((count, count), np.float32)
    matrix[np.arange(count), source] = 1.0
    return matrix.astype(jnp.bfloat16)


def exact(matrix, rows):
    return jnp.dot(matrix, rows, preferred_element_type=jnp.float32).astype(jnp.bfloat16)


def keep(array):
    return pltpu.with_memory_space_constraint(array, pltpu.HBM)


def copy_all(pairs, sems):
    copies = [pltpu.make_async_copy(src, dst, sems.at[i]) for i, (src, dst) in enumerate(pairs)]
    for copy in copies:
        copy.start()
    return copies


def prepare_kernel(
    planes, vel_hbm, dens_hbm, mat_hbm, send_ref, dens16_ref, vel_ref, dens_ref, mat_ref, sems
):
    copies = copy_all([(dens_hbm, dens_ref), (vel_hbm, vel_ref), (mat_hbm, mat_ref)], sems)
    comps, depth, modes = vel_ref.shape
    tiles = modes // LANES
    step = GROUP * planes
    chunk = comps * planes * tiles * GROUP // 2
    copies[0].wait()
    dens16_ref[...] = dens_ref[...].astype(jnp.bfloat16)
    copies[1].wait()
    copies[2].wait()
    for b in range(depth // step):
        parts = []
        for c in range(comps):
            rows = vel_ref[c, pl.ds(b * step, step), :]
            for h in range(tiles):
                parts.append(rows[:, h * LANES : (h + 1) * LANES])
        mixed = exact(mat_ref[...], jnp.concatenate(parts, axis=0))
        for g in range(2):
            send_ref[g, pl.ds(b * chunk, chunk), :] = mixed[g * chunk : (g + 1) * chunk]


def stencil_kernel(
    dens_hbm, other_ref, near_ref, far_ref, near_other_ref, far_other_ref,
    table_hbm, sign_hbm, in_hbm,
    gx_ref, gy_ref, gz_ref, base_ref, field_ref, table_ref, sign_ref, in_ref, zz_ref, sems,
):
    planes, rows, cells = dens_hbm.shape
    here, there = pl.ds(0, cells), pl.ds(cells, cells)
    core = lax.axis_index("grp")
    copies = copy_all(
        [
            (dens_hbm, zz_ref.at[pl.ds(planes, planes), :, here]),
            (table_hbm.at[core], table_ref), (sign_hbm, sign_ref), (in_hbm, in_ref),
        ],
        sems,
    )
    zz_ref[pl.ds(planes, planes), :, there] = other_ref[...]
    odd = lax.axis_index(("row", "col")) % 2
    near_at, far_at = pl.ds(2 * planes * (1 - odd), planes), pl.ds(2 * planes * odd, planes)
    zz_ref[near_at, :, here] = near_ref[...].astype(jnp.float32)
    zz_ref[near_at, :, there] = near_other_ref[...].astype(jnp.float32)
    zz_ref[far_at, :, here] = far_ref[...].astype(jnp.float32)
    zz_ref[far_at, :, there] = far_other_ref[...].astype(jnp.float32)
    copies[0].wait()
    span = 2 * cells
    owned = planes // 2

    def one(p):
        at = planes + owned * core + p
        field = zz_ref[at]
        field_ref[p] = field
        grad_x = grad_y = grad_z = lap = None
        for reach in range(1, 5):
            ahead_x = pltpu.roll(field, span - reach, 1)
            behind_x = pltpu.roll(field, reach, 1)
            ahead_y = pltpu.roll(field, rows - reach, 0)
            behind_y = pltpu.roll(field, reach, 0)
            ahead_z = zz_ref[at + reach]
            behind_z = zz_ref[at - reach]
            a = step_value * first_coef[reach - 1]
            b = step_value * kappa_value * second_coef[reach - 1]
            total = (ahead_x + behind_x) + (ahead_y + behind_y) + (ahead_z + behind_z)
            if reach == 1:
                grad_x = a * (ahead_x - behind_x)
                grad_y = a * (ahead_y - behind_y)
                grad_z = a * (ahead_z - behind_z) + step_value * strat_value
                lap = (1.0 + step_value * kappa_value * 3.0 * centre_coef) * field + b * total
            else:
                grad_x = grad_x + a * (ahead_x - behind_x)
                grad_y = grad_y + a * (ahead_y - behind_y)
                grad_z = grad_z + a * (ahead_z - behind_z)
                lap = lap + b * total
        gx_ref[p] = grad_x
        gy_ref[p] = grad_y
        gz_ref[p] = grad_z
        base_ref[p] = lap

    if rows <= GROUP:
        for p in range(owned):
            one(p)
    else:
        lax.fori_loop(0, owned, lambda p, _: (one(p), 0)[1], 0)
    for copy in copies[1:]:
        copy.wait()


def advance_kernel(
    scale, live_ref, recv_ref, table_ref, sign_ref, in_mat_ref,
    dens_ref, gx_ref, gy_ref, gz_ref, base_ref, mine_ref, give_ref, send_ref, fine_ref,
):
    owned, rows, span = dens_ref.shape
    cells = span // 2
    modes = table_ref.shape[0]
    tiles = modes // (2 * LANES)
    comps = 3
    chunk = comps * owned * tiles * GROUP
    per_tile = chunk // tiles
    sign = sign_ref[0:1, :]
    first_plane = owned * lax.axis_index("grp")
    for b in range(rows // GROUP):
        lanes = [recv_ref[g, pl.ds(b * chunk, chunk), :] for g in range(2)]
        mixed = jnp.dot(
            in_mat_ref[...], jnp.concatenate(lanes, axis=1), preferred_element_type=jnp.float32
        )
        coarse = jnp.concatenate(
            [mixed[h * per_tile : (h + 1) * per_tile] for h in range(tiles)], axis=1
        )
        both = jnp.concatenate([coarse, coarse * sign], axis=0).astype(jnp.bfloat16)
        fine_ref[...] = jnp.dot(both, table_ref[...], preferred_element_type=jnp.float32)
        here = pl.ds(b * GROUP, GROUP)
        parts = []
        for side, out_ref in enumerate((mine_ref, give_ref)):
            for p in range(owned):
                at = (p, here, pl.ds(side * cells, cells))
                vel = [
                    fine_ref[pl.ds(((side * comps + c) * owned + p) * GROUP, GROUP), :]
                    for c in range(comps)
                ]
                moved = base_ref[at] - (
                    vel[0] * gx_ref[at] + vel[1] * gy_ref[at] + vel[2] * gz_ref[at]
                )
                value = jnp.where(first_plane + p < live_ref[0], moved, dens_ref[at])
                out_ref[p, here, :] = value
                parts.append(value.astype(jnp.bfloat16))
        lifted = lax.dot_general(
            jnp.concatenate(parts, axis=0), table_ref[...], (((1,), (1,)), ((), ())),
            preferred_element_type=jnp.float32,
        )
        half = owned * GROUP
        lifted = scale * lifted[:half] + (scale * sign) * lifted[half:]
        for p in range(owned):
            for h in range(tiles):
                for g in range(2):
                    first = b * GROUP * 2 * owned * tiles + (g * owned + p) * tiles + h
                    send_ref[pl.ds(first, GROUP, stride=2 * owned * tiles), :] = lifted[
                        p * GROUP : (p + 1) * GROUP, (2 * h + g) * LANES : (2 * h + g + 1) * LANES
                    ]


def finish_kernel(mine_ref, got_ref, home_ref, next_hbm, buoyancy_hbm, sems):
    owned = mine_ref.shape[0]
    core = lax.axis_index("grp")
    for copy in copy_all(
        [
            (mine_ref, next_hbm.at[pl.ds(owned * core, owned)]),
            (got_ref, next_hbm.at[pl.ds(owned * (1 - core), owned)]),
            (home_ref, buoyancy_hbm),
        ],
        sems,
    ):
        copy.wait()


def per_device(velocity, density, live_planes):
    comps, depth, _, modes = velocity.shape
    planes, rows, cells = density.shape
    slabs = depth // planes
    tiles = modes // LANES
    owned = planes // 2
    fine_cells = 2 * cells
    tables, sign = half_tables(2 * modes, fine_cells)
    sizes = dict(s=GROUP, c=comps, p=owned, h=tiles, y=GROUP, g=2)
    prep_mat = selector("gshcp", "chsgp", sizes)
    in_mat = selector("hcpy", "yhcp", sizes)
    chunk = comps * owned * tiles
    vmem = pl.BlockSpec(memory_space=pltpu.VMEM)
    smem = pl.BlockSpec(memory_space=pltpu.SMEM)
    hbm = pl.BlockSpec(memory_space=pltpu.HBM)
    params = pltpu.CompilerParams(vmem_limit_bytes=(24 if rows <= GROUP else 56) * 2**20)
    f32, b16 = jnp.float32, jnp.bfloat16

    send, dens16 = pl.pallas_call(
        functools.partial(prepare_kernel, planes),
        out_shape=(
            jax.ShapeDtypeStruct((2, slabs * chunk, LANES), b16),
            jax.ShapeDtypeStruct(density.shape, b16),
        ),
        in_specs=[hbm] * 3,
        out_specs=(vmem,) * 2,
        scratch_shapes=[
            pltpu.VMEM((comps, depth, modes), b16),
            pltpu.VMEM(density.shape, f32),
            pltpu.VMEM(prep_mat.shape, b16),
            pltpu.SemaphoreType.DMA((3,)),
        ],
        compiler_params=params,
        name="prepare",
    )(keep(velocity.reshape(comps, depth, modes)), keep(density), keep(prep_mat))

    count = slabs
    even_first = [(i, i ^ 1) for i in range(count)]
    odd_first = [((i + 1) % count, ((i ^ 1) + 1) % count) for i in range(count)]
    pair = [(0, 1), (1, 0)]
    far = lax.ppermute(dens16, ("row", "col"), odd_first)
    near = lax.ppermute(dens16, ("row", "col"), even_first)
    other = lax.ppermute(density, "grp", pair)
    far_other = lax.ppermute(far, "grp", pair)
    near_other = lax.ppermute(near, "grp", pair)
    recv = lax.all_to_all(
        send.reshape(2 * slabs, chunk // 4, 4, LANES), ("grp", "row", "col"), 0, 0, tiled=True
    )
    recv = recv.reshape(2, slabs * chunk, LANES)

    field = jax.ShapeDtypeStruct((owned, rows, fine_cells), f32)
    *grads, table, sign, in_mat = pl.pallas_call(
        stencil_kernel,
        out_shape=(field,) * 5 + (
            jax.ShapeDtypeStruct(tables[0].shape, b16),
            jax.ShapeDtypeStruct(sign.shape, f32),
            jax.ShapeDtypeStruct(in_mat.shape, b16),
        ),
        in_specs=[hbm] + [vmem] * 5 + [hbm] * 3,
        out_specs=(vmem,) * 8,
        scratch_shapes=[
            pltpu.VMEM((3 * planes, rows, fine_cells), f32), pltpu.SemaphoreType.DMA((4,))
        ],
        compiler_params=params,
        cost_estimate=pl.CostEstimate(
            flops=16 * density.size, bytes_accessed=24 * density.size, transcendentals=0
        ),
        name="stencil",
    )(
        keep(density), other, near, far, near_other, far_other,
        keep(tables), keep(sign), keep(in_mat),
    )
    gx, gy, gz, base, dens = grads

    scale = -math.sqrt(2.0 / fine_cells)
    half_field = jax.ShapeDtypeStruct((owned, rows, cells), f32)
    mine, give, back = pl.pallas_call(
        functools.partial(advance_kernel, scale),
        out_shape=(
            half_field, half_field,
            jax.ShapeDtypeStruct((rows * 2 * owned * tiles, LANES), f32),
        ),
        in_specs=[smem] + [vmem] * 9,
        out_specs=(vmem,) * 3,
        scratch_shapes=[pltpu.VMEM((2 * comps * owned * GROUP, cells), f32)],
        compiler_params=params,
        name="advance",
    )(live_planes, recv, table, sign, in_mat, dens, gx, gy, gz, base)

    home = lax.all_to_all(
        back.reshape(2 * rows * owned, 1, modes), ("row", "col", "grp"), 0, 0, tiled=True
    )
    got = lax.ppermute(give, "grp", pair)
    return pl.pallas_call(
        finish_kernel,
        out_shape=(
            jax.ShapeDtypeStruct(density.shape, f32),
            jax.ShapeDtypeStruct((depth, 1, modes), f32),
        ),
        in_specs=[vmem] * 3,
        out_specs=(hbm,) * 2,
        scratch_shapes=[pltpu.SemaphoreType.DMA((3,))],
        compiler_params=params,
        name="finish",
    )(mine, got, home)


def solution(mesh):
    in_specs = (
        P(None, None, ("row", "col"), "grp"),
        P(("row", "col"), None, "grp"),
        P(("row", "col")),
    )
    out_specs = (P(("row", "col"), None, "grp"), P(None, ("row", "col"), "grp"))
    return jax.shard_map(
        per_device, mesh=mesh, in_specs=in_specs, out_specs=out_specs, check_vma=False
    )
```

```python
import functools
import math

import jax
import jax.numpy as jnp
import numpy as np
from jax import lax
from jax.experimental import pallas as pl
from jax.experimental.pallas import tpu as pltpu
from jax.sharding import PartitionSpec as P

first_coef = (4.0 / 5.0, -1.0 / 5.0, 4.0 / 105.0, -1.0 / 280.0)
second_coef = (8.0 / 5.0, -1.0 / 5.0, 8.0 / 315.0, -1.0 / 560.0)
centre_coef = -205.0 / 72.0
kappa_value = 0.1
step_value = 0.2
strat_value = 1.0

LANES = 128
GROUP = 16


def half_tables(mode_count, fine_cells):
    k = np.arange(mode_count)
    half = mode_count // 2
    frequency = np.where(k < half, k, k - half + 1)
    phase = frequency[:, None] * np.arange(fine_cells)[None, :] % fine_cells
    angle = phase.astype(np.float32) * np.float32(2.0 * math.pi / fine_cells)
    table = np.where((k < half)[:, None], np.cos(angle), np.sin(angle)).astype(np.float32)
    order = k.reshape(2, half // LANES, LANES).transpose(1, 0, 2).reshape(-1)
    table = table[order].reshape(mode_count, 2, fine_cells // 2).transpose(1, 0, 2)
    sign = np.where(frequency[order] % 2 == 0, 1.0, -1.0).astype(np.float32)
    return np.ascontiguousarray(table).astype(jnp.bfloat16), np.tile(sign, (8, 1))


def selector(out_axes, in_axes, sizes):
    count = math.prod(sizes[a] for a in in_axes)
    index = np.arange(count).reshape([sizes[a] for a in in_axes])
    source = index.transpose([in_axes.index(a) for a in out_axes]).reshape(-1)
    matrix = np.zeros((count, count), np.float32)
    matrix[np.arange(count), source] = 1.0
    return matrix.astype(jnp.bfloat16)


def exact(matrix, rows):
    return jnp.dot(matrix, rows, preferred_element_type=jnp.float32).astype(jnp.bfloat16)


def keep(array):
    return pltpu.with_memory_space_constraint(array, pltpu.HBM)


def copy_all(pairs, sems):
    copies = [pltpu.make_async_copy(src, dst, sems.at[i]) for i, (src, dst) in enumerate(pairs)]
    for copy in copies:
        copy.start()
    return copies


def prepare_kernel(
    planes, vel_hbm, dens_hbm, mat_hbm,
    send_hbm, dens16_ref, dens_ref, give_ref, vel_ref, mat_ref, send_ref, sems,
):
    copies = copy_all([(dens_hbm, dens_ref), (vel_hbm, vel_ref), (mat_hbm, mat_ref)], sems)
    copies[0].wait()
    dens16_ref[...] = dens_ref[...].astype(jnp.bfloat16)
    owned = planes // 2
    give_ref[...] = dens_ref[pl.ds(owned * (1 - lax.axis_index("grp")), owned)]
    copies[1].wait()
    copies[2].wait()
    pl.when(lax.axis_index("col") == 0)(
        lambda: order_velocity(planes, vel_ref, mat_ref, send_ref, send_hbm, sems.at[0])
    )


def order_kernel(planes, vel_ref, mat_ref, unused_hbm, send_hbm, send_ref, sem):
    pl.when(lax.axis_index("col") != 0)(
        lambda: order_velocity(planes, vel_ref, mat_ref, send_ref, send_hbm, sem)
    )


def order_velocity(planes, vel_ref, mat_ref, send_ref, send_hbm, sem):
    comps, depth, modes = vel_ref.shape
    tiles = modes // LANES
    step = GROUP * planes
    chunk = comps * planes * tiles * GROUP // 2
    for b in range(depth // step):
        parts = []
        for c in range(comps):
            rows = vel_ref[c, pl.ds(b * step, step), :]
            for h in range(tiles):
                parts.append(rows[:, h * LANES : (h + 1) * LANES])
        mixed = exact(mat_ref[...], jnp.concatenate(parts, axis=0))
        for g in range(2):
            send_ref[g, pl.ds(b * chunk, chunk), :] = mixed[g * chunk : (g + 1) * chunk]
    copy = pltpu.make_async_copy(send_ref, send_hbm, sem)
    copy.start()
    copy.wait()


def local_kernel(
    dens_ref, other_ref, live_ref, table_hbm, sign_hbm, in_hbm,
    gx_ref, gy_ref, base_ref, mask_ref, table_ref, sign_ref, in_ref, sems,
):
    planes, rows, cells = dens_ref.shape
    core = lax.axis_index("grp")
    copies = copy_all(
        [(table_hbm.at[core], table_ref), (sign_hbm, sign_ref), (in_hbm, in_ref)], sems
    )
    owned = planes // 2

    def one(p):
        at = owned * core + p
        field = jnp.concatenate([dens_ref[at], other_ref[p]], axis=1)
        live = (at < live_ref[0]).astype(jnp.float32)
        grad_x, grad_y, lap = differences(
            lambda m: pltpu.roll(field, (-m) % (2 * cells), 1),
            lambda m: pltpu.roll(field, (-m) % rows, 0),
        )
        mask_ref[p] = jnp.broadcast_to(live, mask_ref.shape[1:])
        gx_ref[p] = live * grad_x
        gy_ref[p] = live * grad_y
        base_ref[p] = field + live * (
            (step_value * kappa_value * 3.0 * centre_coef) * field + lap
        )

    loop_planes(owned, rows, one)
    for copy in copies:
        copy.wait()


def halo_kernel(far_ref, near_ref, dens_ref, mine_ref, give_ref, zz_ref):
    planes = dens_ref.shape[0]
    odd = lax.axis_index(("row", "col")) % 2
    zz_ref[pl.ds(2 * planes * (1 - odd), planes)] = near_ref[...].astype(jnp.float32)
    zz_ref[pl.ds(2 * planes * odd, planes)] = far_ref[...].astype(jnp.float32)
    zz_ref[pl.ds(planes, planes)] = dens_ref[...]
    owned = planes // 2
    core = lax.axis_index("grp")

    for out_ref, first in ((mine_ref, owned * core), (give_ref, owned * (1 - core))):

        def one(p):
            grad_z, lap = differences(lambda m: zz_ref[planes + first + p + m])
            out_ref[0, p] = (grad_z + step_value * strat_value).astype(out_ref.dtype)
            out_ref[1, p] = lap.astype(out_ref.dtype)

        loop_planes(owned, dens_ref.shape[1], one)


def differences(*shifted):
    grads = [None] * len(shifted)
    lap = None
    for reach in range(1, 5):
        a = step_value * first_coef[reach - 1]
        b = step_value * kappa_value * second_coef[reach - 1]
        total = None
        for i, shift in enumerate(shifted):
            ahead, behind = shift(reach), shift(-reach)
            grad, pair = a * (ahead - behind), ahead + behind
            grads[i] = grad if reach == 1 else grads[i] + grad
            total = pair if total is None else total + pair
        lap = b * total if reach == 1 else lap + b * total
    return (*grads, lap)


def loop_planes(count, rows, body):
    if rows <= GROUP:
        for p in range(count):
            body(p)
    else:
        lax.fori_loop(0, count, lambda p, _: (body(p), 0)[1], 0)


def advance_kernel(
    scale, recv_ref, table_ref, sign_ref, in_mat_ref, gx_ref, gy_ref, base_ref, mask_ref,
    z_mine_ref, z_other_ref, mine_ref, give_ref, send_ref, fine_ref,
):
    owned, rows, span = base_ref.shape
    cells = span // 2
    modes = table_ref.shape[0]
    tiles = modes // (2 * LANES)
    comps = 3
    chunk = comps * owned * tiles * GROUP
    per_tile = chunk // tiles
    sign = sign_ref[0:1, :]
    for b in range(rows // GROUP):
        lanes = [recv_ref[g, pl.ds(b * chunk, chunk), :] for g in range(2)]
        mixed = jnp.dot(
            in_mat_ref[...], jnp.concatenate(lanes, axis=1), preferred_element_type=jnp.float32
        )
        coarse = jnp.concatenate(
            [mixed[h * per_tile : (h + 1) * per_tile] for h in range(tiles)], axis=1
        )
        both = jnp.concatenate([coarse, coarse * sign], axis=0).astype(jnp.bfloat16)
        fine_ref[...] = jnp.dot(both, table_ref[...], preferred_element_type=jnp.float32)
        here = pl.ds(b * GROUP, GROUP)
        parts = []
        for side, (out_ref, z_ref) in enumerate(
            ((mine_ref, z_mine_ref), (give_ref, z_other_ref))
        ):
            for p in range(owned):
                at = (p, here, pl.ds(side * cells, cells))
                vel = [
                    fine_ref[pl.ds(((side * comps + c) * owned + p) * GROUP, GROUP), :]
                    for c in range(comps)
                ]
                grad_z, lap_z = (z_ref[i, p, here, :].astype(jnp.float32) for i in range(2))
                along_z = vel[2] * grad_z - lap_z
                value = base_ref[at] - (
                    vel[0] * gx_ref[at] + vel[1] * gy_ref[at]
                    + mask_ref[p, :, pl.ds(side * cells, cells)] * along_z
                )
                out_ref[p, here, :] = value
                parts.append(value.astype(jnp.bfloat16))
        lifted = lax.dot_general(
            jnp.concatenate(parts, axis=0), table_ref[...], (((1,), (1,)), ((), ())),
            preferred_element_type=jnp.float32,
        )
        half = owned * GROUP
        lifted = scale * lifted[:half] + (scale * sign) * lifted[half:]
        for p in range(owned):
            for h in range(tiles):
                for g in range(2):
                    first = b * GROUP * 2 * owned * tiles + (g * owned + p) * tiles + h
                    send_ref[pl.ds(first, GROUP, stride=2 * owned * tiles), :] = lifted[
                        p * GROUP : (p + 1) * GROUP, (2 * h + g) * LANES : (2 * h + g + 1) * LANES
                    ]


def finish_kernel(mine_ref, got_ref, home_ref, next_hbm, buoyancy_hbm, sems):
    owned = mine_ref.shape[0]
    core = lax.axis_index("grp")
    for copy in copy_all(
        [
            (mine_ref, next_hbm.at[pl.ds(owned * core, owned)]),
            (got_ref, next_hbm.at[pl.ds(owned * (1 - core), owned)]),
            (home_ref, buoyancy_hbm),
        ],
        sems,
    ):
        copy.wait()


def per_device(velocity, density, live_planes):
    comps, depth, _, modes = velocity.shape
    planes, rows, cells = density.shape
    slabs = depth // planes
    tiles = modes // LANES
    owned = planes // 2
    fine_cells = 2 * cells
    tables, sign = half_tables(2 * modes, fine_cells)
    sizes = dict(s=GROUP, c=comps, p=owned, h=tiles, y=GROUP, g=2)
    prep_mat = selector("gshcp", "chsgp", sizes)
    in_mat = selector("hcpy", "yhcp", sizes)
    chunk = comps * owned * tiles
    vmem = pl.BlockSpec(memory_space=pltpu.VMEM)
    smem = pl.BlockSpec(memory_space=pltpu.SMEM)
    hbm = pl.BlockSpec(memory_space=pltpu.HBM)
    params = pltpu.CompilerParams(vmem_limit_bytes=(24 if rows <= GROUP else 56) * 2**20)
    f32, b16 = jnp.float32, jnp.bfloat16

    half_field = jax.ShapeDtypeStruct((owned, rows, cells), f32)
    send_shape = (2, slabs * chunk, LANES)
    send, dens16, dens, give, vel, mat = pl.pallas_call(
        functools.partial(prepare_kernel, planes),
        out_shape=(
            pltpu.HBM(send_shape, b16),
            jax.ShapeDtypeStruct(density.shape, b16),
            jax.ShapeDtypeStruct(density.shape, f32),
            half_field,
            jax.ShapeDtypeStruct((comps, depth, modes), b16),
            jax.ShapeDtypeStruct(prep_mat.shape, b16),
        ),
        in_specs=[hbm] * 3,
        out_specs=(hbm,) + (vmem,) * 5,
        scratch_shapes=[pltpu.VMEM(send_shape, b16), pltpu.SemaphoreType.DMA((3,))],
        compiler_params=params,
        name="prepare",
    )(keep(velocity.reshape(comps, depth, modes)), keep(density), keep(prep_mat))
    send = pl.pallas_call(
        functools.partial(order_kernel, planes),
        out_shape=jax.ShapeDtypeStruct(send_shape, b16),
        in_specs=[vmem, vmem, hbm],
        out_specs=hbm,
        input_output_aliases={2: 0},
        scratch_shapes=[pltpu.VMEM(send_shape, b16), pltpu.SemaphoreType.DMA],
        compiler_params=params,
        name="order",
    )(vel, mat, keep(send))

    count = slabs
    even_first = [(i, i ^ 1) for i in range(count)]
    odd_first = [((i + 1) % count, ((i ^ 1) + 1) % count) for i in range(count)]
    pair = [(0, 1), (1, 0)]
    near = lax.ppermute(dens16, ("row", "col"), even_first)
    far = lax.ppermute(dens16, ("row", "col"), odd_first)
    other = lax.ppermute(give, "grp", pair)
    recv = lax.all_to_all(
        send.reshape(2 * slabs, chunk // 4, 4, LANES), ("grp", "row", "col"), 0, 0, tiled=True
    )
    recv = recv.reshape(2, slabs * chunk, LANES)

    z_shape = (2, owned, rows, cells)
    z_mine, z_give = pl.pallas_call(
        halo_kernel,
        out_shape=(jax.ShapeDtypeStruct(z_shape, f32), jax.ShapeDtypeStruct(z_shape, b16)),
        in_specs=[vmem] * 3,
        out_specs=(vmem,) * 2,
        scratch_shapes=[pltpu.VMEM((3 * planes, rows, cells), f32)],
        compiler_params=params,
        cost_estimate=pl.CostEstimate(
            flops=16 * density.size, bytes_accessed=16 * density.size, transcendentals=0
        ),
        name="halo",
    )(far, near, dens)
    z_other = lax.ppermute(z_give, "grp", pair)

    field = jax.ShapeDtypeStruct((owned, rows, fine_cells), f32)
    gx, gy, base, mask, table, sign, in_mat = pl.pallas_call(
        local_kernel,
        out_shape=(field,) * 3 + (
            jax.ShapeDtypeStruct((owned, 1, fine_cells), f32),
            jax.ShapeDtypeStruct(tables[0].shape, b16),
            jax.ShapeDtypeStruct(sign.shape, f32),
            jax.ShapeDtypeStruct(in_mat.shape, b16),
        ),
        in_specs=[vmem, vmem, smem] + [hbm] * 3,
        out_specs=(vmem,) * 7,
        scratch_shapes=[pltpu.SemaphoreType.DMA((3,))],
        compiler_params=params,
        cost_estimate=pl.CostEstimate(
            flops=16 * density.size, bytes_accessed=24 * density.size, transcendentals=0
        ),
        name="local",
    )(dens, other, live_planes, keep(tables), keep(sign), keep(in_mat))

    scale = -math.sqrt(2.0 / fine_cells)
    mine, give, back = pl.pallas_call(
        functools.partial(advance_kernel, scale),
        out_shape=(
            half_field, half_field,
            jax.ShapeDtypeStruct((rows * 2 * owned * tiles, LANES), f32),
        ),
        in_specs=[vmem] * 10,
        out_specs=(vmem,) * 3,
        scratch_shapes=[pltpu.VMEM((2 * comps * owned * GROUP, cells), f32)],
        compiler_params=params,
        name="advance",
    )(recv, table, sign, in_mat, gx, gy, base, mask, z_mine, z_other)

    home = lax.all_to_all(
        back.reshape(2 * rows * owned, 1, modes), ("row", "col", "grp"), 0, 0, tiled=True
    )
    got = lax.ppermute(give, "grp", pair)
    return pl.pallas_call(
        finish_kernel,
        out_shape=(
            jax.ShapeDtypeStruct(density.shape, f32),
            jax.ShapeDtypeStruct((depth, 1, modes), f32),
        ),
        in_specs=[vmem] * 3,
        out_specs=(hbm,) * 2,
        scratch_shapes=[pltpu.SemaphoreType.DMA((3,))],
        compiler_params=params,
        name="finish",
    )(mine, got, home)


def solution(mesh):
    in_specs = (
        P(None, None, ("row", "col"), "grp"),
        P(("row", "col"), None, "grp"),
        P(("row", "col")),
    )
    out_specs = (P(("row", "col"), None, "grp"), P(None, ("row", "col"), "grp"))
    return jax.shard_map(
        per_device, mesh=mesh, in_specs=in_specs, out_specs=out_specs, check_vma=False
    )
```
